32 devices in a mesh: cohort: 2 (over x), grp: 4 (over z), vox: 4 (over y, core).
Axes of the slice: x: 2, y: 2, z: 4, core: 2. Of those that a mesh axis runs over, the one named last changes fastest.
Arguments:
- probes: bfloat16 [16384, 256], P(('cohort', 'grp', 'vox')), parts along dimension 0, may hold values from -6 to 6
- blocks: bfloat16 [512, 4, 128, 128], P(('cohort', 'grp', 'vox')), parts along dimension 0, may hold values from -0.25 to 0.25
- pattern: int32 [512, 4], P(('cohort', 'grp', 'vox')), parts along dimension 0, may hold values from 0 to 31, as said below
- scale_exp: int32 [512, 4], P(('cohort', 'grp', 'vox')), parts along dimension 0, may hold values from -2 to 2
- noise: float32 [512, 128], P(('cohort', 'grp', 'vox')), parts along dimension 0, may hold values from 0.1 to 1
Outputs:
- hessian_probes: float32 [16384, 256], P(('cohort', 'grp', 'vox')), parts along dimension 0
The draws below stay inside these ranges and needn't reach their ends.
There are 2 independent parts, one for each index of `cohort`. The reference program is written for one: setup_inputs(seed, part) draws one part's arguments, and reference() takes and returns one part's arrays. A program takes and returns all parts, laid end to end along the dimension named above; each array names one. Nothing has to cross between parts.
Inputs may be any that keep to these rules, and one draw needn't show every extreme that they name: pattern is below 16 in the last group's rows; other rows may reach into the next group's parameter blocks.
All inputs are finite; a program needn't handle non-finite values.
Results may differ from the reference program's by a relative error of at most 0.0016.
Values may be sent and summed in bfloat16 or wider, within the bound.
A program may use at most 128 MiB of HBM per device.

```python
import math
import jax
import jax.numpy as jnp
from jax import lax

BLK = 128
PROBES = 256
NNZ = 4
ROWS_DEV = 16
GROUP_BLOCKS = 16
PARAM_BLOCKS = 64
PARAMS = 8192
BLOCK_ROWS = 256
N_GRP = 4
N_VOX = 4


def draw_pattern(key, part):
    rows = jnp.arange(BLOCK_ROWS)
    group_id = rows // (ROWS_DEV * N_VOX)
    reach = jnp.where(group_id == N_GRP - 1, GROUP_BLOCKS, 2 * GROUP_BLOCKS)
    raw = jax.random.randint(key, (BLOCK_ROWS, NNZ), 0, 1 << 20)
    columns = raw % reach[:, None]
    columns = columns.at[0, 0].set(2 * GROUP_BLOCKS - 1).at[0, 1].set(0)
    return columns.astype(jnp.int32)


def place_ends(result, stream_key, smallest, top_value):
    dims = result.shape
    place = [jax.random.randint(jax.random.fold_in(stream_key, axis), (), 0, dims[axis]) for axis in range(len(dims))]
    result = result.at[tuple(place)].set(smallest)
    longest = dims.index(max(dims))
    place[longest] = (place[longest] + 1) % dims[longest]
    return result.at[tuple(place)].set(top_value)


def block_scale(stream_key, shape, split, least, top_value):
    def one(position, shards_of):
        heights = jax.random.uniform(jax.random.fold_in(jax.random.fold_in(stream_key, 6), position), (shards_of,), jnp.float32, least / len(split), top_value / len(split))
        return jnp.repeat(jnp.exp(heights), shape[position] // shards_of).reshape((-1,) + (1,) * (len(shape) - position - 1))

    gain = one(*split[0])
    for cut in split[1:]:
        gain = gain * one(*cut)
    return gain


def gaussian(own_key, shape, deviation, most, cuts=(), dtype=jnp.bfloat16):
    entries = deviation * jax.random.normal(own_key, shape, jnp.float32)
    if cuts:
        entries = entries * block_scale(own_key, shape, cuts, -0.22, 0.18)
    return jnp.clip(entries, -most, most).astype(dtype)


def setup_inputs(seed: int = 0, part: int = 0) -> dict:
    seeds = jax.random.split(jax.random.key(seed), 6)
    part_splits = jax.random.split(jax.random.fold_in(seeds[5], part), 6)
    probes = gaussian(part_splits[0], (PARAMS, PROBES), 1.0, 6.0, ((0, 16),))
    blocks = gaussian(part_splits[1], (BLOCK_ROWS, NNZ, BLK, BLK), (BLK * NNZ) ** -0.5, 0.25, ((0, 16),))
    pattern = draw_pattern(jax.random.fold_in(jax.random.fold_in(seeds[5], part), 71), part)
    scale_exp = place_ends(jax.random.randint(part_splits[3], (BLOCK_ROWS, NNZ), -2, 3), jax.random.fold_in(part_splits[3], 1), -2, 2).astype(jnp.int32)
    noise = jnp.clip(jnp.exp(math.log(1.0) - 2.3025851 * jax.random.uniform(part_splits[4], (BLOCK_ROWS, BLK), jnp.float32) ** block_scale(part_splits[4], (BLOCK_ROWS, BLK), ((0, 16),), -0.2, 0.2)), 0.1, 1.0)
    return dict(probes=probes, blocks=blocks, pattern=pattern, scale_exp=scale_exp, noise=noise)


def reference(probes, blocks, pattern, scale_exp, noise):
    panels = probes.reshape(PARAM_BLOCKS, BLK, PROBES)
    devices_all = N_GRP * N_VOX
    group_of = (jnp.arange(devices_all) // N_VOX).astype(jnp.int32)
    items = (blocks.reshape(devices_all, ROWS_DEV, NNZ, BLK, BLK),
             pattern.reshape(devices_all, ROWS_DEV, NNZ),
             scale_exp.reshape(devices_all, ROWS_DEV, NNZ),
             noise.reshape(devices_all, ROWS_DEV, BLK),
             group_of)

    def step(total, item):
        block_vals, local_cols, expo, weights, group_id = item
        columns = (local_cols + group_id * GROUP_BLOCKS).astype(jnp.int32)
        scales = jnp.exp2(expo.astype(jnp.float32))
        forward = jnp.zeros((ROWS_DEV, BLK, PROBES), jnp.float32)
        for slot in range(NNZ):
            picked = panels[columns[:, slot]].astype(jnp.float32)
            product = jnp.einsum("rab,rbk->rak", block_vals[:, slot].astype(jnp.float32), picked)
            forward = forward + product * scales[:, slot, None, None]
        weighted = (weights[:, :, None] * forward).astype(jnp.bfloat16)
        weighted = lax.optimization_barrier(weighted).astype(jnp.float32)
        for slot in range(NNZ):
            back = jnp.einsum("rab,rak->rbk", block_vals[:, slot].astype(jnp.float32), weighted)
            total = total.at[columns[:, slot]].add(back * scales[:, slot, None, None])
        return total, None

    start = jnp.zeros((PARAM_BLOCKS, BLK, PROBES), jnp.float32)
    total = lax.scan(step, start, items)[0]
    return total.reshape(PARAMS, PROBES)
```

```python
import functools

import jax
import jax.numpy as jnp
from jax import lax
from jax.experimental import pallas as pl
from jax.experimental.pallas import tpu as pltpu
from jax.sharding import PartitionSpec as P

MESH = pl.DeviceIdType.MESH


def kernel(
    groups, voxes, pattern, scale_exp, links, probes, blocks, noise, out,
    panels, chain, core_out, core_in, far_out, far_in,
    near_send, near_recv, y_send, y_recv, z_send, z_recv,
    pair_send, pair_recv, far_send, far_recv,
):
    rows_here, count, width = blocks.shape[0], blocks.shape[1], blocks.shape[2]
    held = probes.shape[0]
    ys = voxes // 2
    entries = rows_here * count
    cohort, grp, vox = lax.axis_index("cohort"), lax.axis_index("grp"), lax.axis_index("vox")
    y, core = vox // 2, lax.rem(vox, 2)
    before = lax.rem(grp + groups - 1, groups)
    after = lax.rem(grp + 1, groups)
    mate = (cohort, grp, 2 * y + 1 - core)

    def column(d):
        return lax.rem(y + d, ys)

    def device(group, d):
        return (cohort, group, 2 * column(d) + core)

    def shard(half, index):
        return panels.at[pl.ds((half * voxes + index) * held, held)]

    def remote(src, dst, send, recv, to):
        return pltpu.make_async_remote_copy(
            src_ref=src, dst_ref=dst, send_sem=send, recv_sem=recv, device_id=to, device_id_type=MESH
        )

    barrier = pltpu.get_barrier_semaphore()
    greeted = [mate] + [device(grp, d) for d in range(1, ys)]
    greeted += [device(group, d) for group in (before, after) for d in range(ys)]
    for other in greeted:
        pl.semaphore_signal(barrier, inc=1, device_id=other, device_id_type=MESH)
    pl.semaphore_wait(barrier, len(greeted))

    started = []

    def start(copy):
        copy.start()
        started.append(copy)

    for d in range(ys - 1, -1, -1):
        start(remote(probes, shard(1, vox), z_send.at[d], z_recv.at[d], device(before, d)))
    for d in range(1, ys):
        start(remote(probes, shard(0, vox), y_send.at[d - 1], y_recv.at[d - 1], device(grp, d)))
    start(remote(probes, shard(0, vox), near_send.at[0], near_recv.at[0], mate))
    panels[pl.ds(vox * held, held)] = probes[...]

    arrivals = []
    for d in range(1, ys):
        arrivals.append((0, d, y_send.at[d - 1], y_recv.at[d - 1]))
    for d in range(ys):
        arrivals.append((1, d, z_send.at[d], z_recv.at[d]))
    for place, (half, d, send, recv) in enumerate(arrivals):
        origin = 2 * lax.rem(y + ys - d, ys) + core
        slot = shard(half, origin)
        remote(slot, slot, send, recv, mate).wait_recv()
        start(remote(slot, slot, near_send.at[place + 1], near_recv.at[place + 1], mate))
    mates = [(0, 0)] + [(half, d) for half, d, _, _ in arrivals]
    for place, (half, d) in enumerate(mates):
        origin = 2 * lax.rem(y + ys - d, ys) + 1 - core
        slot = shard(half, origin)
        remote(slot, slot, near_send.at[place], near_recv.at[place], mate).wait_recv()

    def row(r, carry):
        scaled, picked = [], []
        for n in range(count):
            scale = lax.shift_left(jnp.int32(1), scale_exp[r * count + n] + 2).astype(jnp.float32) * 0.25
            scaled.append((blocks[r, n].astype(jnp.float32) * scale).astype(jnp.bfloat16))
            picked.append(panels[pattern[r * count + n]])
        left = jnp.concatenate(scaled, axis=1)
        forward = jnp.dot(left, jnp.concatenate(picked, axis=0), preferred_element_type=jnp.float32)
        weight = jnp.transpose(jnp.broadcast_to(noise[pl.ds(r, 1), :], (width, width)))
        weight = jnp.concatenate([weight] * (forward.shape[1] // width), axis=1)
        weighted = (weight * forward).astype(jnp.bfloat16)
        back = lax.dot_general(
            left, weighted, (((0,), (0,)), ((), ())), preferred_element_type=jnp.float32
        )
        for n in range(count):
            link = links[r * count + n]
            earlier = jnp.where(link >= 0, chain[jnp.maximum(link, 0)], 0.0)
            chain[r * count + n] = back[n * width : (n + 1) * width] + earlier
        return carry

    lax.fori_loop(0, rows_here, row, 0)

    def total(half, index, k):
        link = links[entries + (half * voxes + index) * held + k]
        return jnp.where(link >= 0, chain[jnp.maximum(link, 0)], 0.0)

    order = [(1, d) for d in range(ys - 1, -1, -1)] + [(0, d) for d in range(ys - 1, -1, -1)]
    for half, d in order:
        place = half * ys + d
        for k in range(held):
            core_out[place, k] = total(half, 2 * column(d) + 1 - core, k)
        start(remote(core_out.at[place], core_in.at[place], pair_send.at[place], pair_recv.at[place], mate))
    for half, d in order:
        place = half * ys + d
        remote(core_out.at[place], core_in.at[place], pair_send.at[place], pair_recv.at[place], mate).wait_recv()
        for k in range(held):
            both = total(half, 2 * column(d) + core, k) + core_in[place, k]
            if half == 0 and d == 0:
                out[k] = both
            else:
                far_out[place - 1, k] = both.astype(jnp.bfloat16)
        if half == 1 or d > 0:
            to = device(after if half else grp, d)
            start(remote(far_out.at[place - 1], far_in.at[place - 1], far_send.at[place - 1], far_recv.at[place - 1], to))
    for half, d in order:
        place = half * ys + d - 1
        if place >= 0:
            remote(far_out.at[place], far_in.at[place], far_send.at[place], far_recv.at[place], mate).wait_recv()
            for k in range(held):
                out[k] += far_in[place, k].astype(jnp.float32)
    for copy in started:
        copy.wait_send()


def solution(mesh):
    groups, voxes = mesh.shape["grp"], mesh.shape["vox"]

    def local(probes, blocks, pattern, scale_exp, noise):
        rows_here, count, width, _ = blocks.shape
        cols = probes.shape[1]
        held = probes.shape[0] // width
        entries = rows_here * count
        ys = voxes // 2
        flat = pattern.reshape(entries)
        numbers = jnp.arange(entries, dtype=jnp.int32)
        wanted = jnp.concatenate([flat, jnp.arange(2 * voxes * held, dtype=jnp.int32)])
        limit = jnp.concatenate([numbers, jnp.full((2 * voxes * held,), entries, jnp.int32)])
        match = (wanted[:, None] == flat[None, :]) & (numbers[None, :] < limit[:, None])
        links = jnp.max(jnp.where(match, numbers[None, :], -1), axis=1)
        smem = pl.BlockSpec(memory_space=pltpu.SMEM)
        vmem = pl.BlockSpec(memory_space=pltpu.VMEM)
        dma = pltpu.SemaphoreType.DMA
        result = pl.pallas_call(
            functools.partial(kernel, groups, voxes),
            out_shape=jax.ShapeDtypeStruct((held, width, cols), jnp.float32),
            in_specs=[smem] * 3 + [vmem] * 3,
            out_specs=vmem,
            scratch_shapes=[
                pltpu.VMEM((2 * voxes * held, width, cols), jnp.bfloat16),
                pltpu.VMEM((entries, width, cols), jnp.float32),
                pltpu.VMEM((2 * ys, held, width, cols), jnp.float32),
                pltpu.VMEM((2 * ys, held, width, cols), jnp.float32),
                pltpu.VMEM((2 * ys - 1, held, width, cols), jnp.bfloat16),
                pltpu.VMEM((2 * ys - 1, held, width, cols), jnp.bfloat16),
                dma((2 * ys,)), dma((2 * ys,)),
                dma((max(ys - 1, 1),)), dma((max(ys - 1, 1),)),
                dma((ys,)), dma((ys,)),
                dma((2 * ys,)), dma((2 * ys,)),
                dma((2 * ys - 1,)), dma((2 * ys - 1,)),
            ],
            compiler_params=pltpu.CompilerParams(
                collective_id=0, has_side_effects=True, vmem_limit_bytes=56 * 1024 * 1024
            ),
        )(flat, scale_exp.reshape(entries), links, probes.reshape(held, width, cols), blocks, noise)
        return result.reshape(held * width, cols)

    in_specs = (
        P(("cohort", "grp", "vox"), None),
        P(("cohort", "grp", "vox"), None, None, None),
        P(("cohort", "grp", "vox"), None),
        P(("cohort", "grp", "vox"), None),
        P(("cohort", "grp", "vox"), None),
    )
    out_specs = P(("cohort", "grp", "vox"), None)
    return jax.shard_map(local, mesh=mesh, in_specs=in_specs, out_specs=out_specs, check_vma=False)
```

```python
import functools

import jax
import jax.numpy as jnp
from jax import lax
from jax.experimental import pallas as pl
from jax.experimental.pallas import tpu as pltpu
from jax.sharding import PartitionSpec as P

MESH = pl.DeviceIdType.MESH


def kernel(
    groups, voxes, scale_exp, pattern, probes, blocks, noise, out,
    panels, split, scaled, weights, chain, tables, other_pattern, other_noise, numbers,
    pair_out, pair_in, far_out, far_in,
    probe_send, probe_recv, mate_send, mate_recv, far_send, far_recv, local_sem,
):
    rows_here, count, width = blocks.shape[0], blocks.shape[1], blocks.shape[2]
    held = probes.shape[0]
    part = probes.shape[2] // 2
    ys = voxes // 2
    entries = rows_here * count
    cohort, grp, vox = lax.axis_index("cohort"), lax.axis_index("grp"), lax.axis_index("vox")
    y, core = vox // 2, lax.rem(vox, 2)
    before = lax.rem(grp + groups - 1, groups)
    after = lax.rem(grp + 1, groups)
    not_first, not_last = grp > 0, grp < groups - 1
    cores = (core, 1 - core)
    mate = (cohort, grp, 2 * y + 1 - core)

    def vox_at(d, q):
        return 2 * lax.rem(y + ys + d, ys) + cores[q]

    def device(group, d, q):
        return (cohort, group, vox_at(d, q))

    def shard(half, index):
        return panels.at[pl.ds((half * voxes + index) * held, held)]

    def remote(src, dst, send, recv, to):
        return pltpu.make_async_remote_copy(
            src_ref=src, dst_ref=dst, send_sem=send, recv_sem=recv, device_id=to, device_id_type=MESH
        )

    def when(condition, act):
        if condition is None:
            act()
        else:
            pl.when(condition)(act)

    places = [(1, d, q) for d in range(ys - 1, -1, -1) for q in (0, 1)]
    places += [(0, d, q) for d in range(ys - 1, 0, -1) for q in (0, 1)]

    barrier = pltpu.get_barrier_semaphore()
    greeted = [(None, mate)] + [(None, device(grp, d, q)) for d in range(1, ys) for q in (0, 1)]
    greeted += [(not_first, device(before, d, q)) for d in range(ys) for q in (0, 1)]
    greeted += [(not_last, device(after, d, q)) for d in range(ys) for q in (0, 1)]
    for condition, one in greeted:
        when(condition, functools.partial(
            pl.semaphore_signal, barrier, inc=1, device_id=one, device_id_type=MESH
        ))
    for j in range(2):
        split[j] = probes[:, :, j * part : (j + 1) * part]
    sides = not_first.astype(jnp.int32) + not_last.astype(jnp.int32)
    pl.semaphore_wait(barrier, 2 * ys - 1 + 2 * ys * sides)

    started = []

    def start(copy, condition=None):
        when(condition, copy.start)
        started.append((condition, copy))

    for place, (half, d, q) in enumerate(places):
        to = device(before if half else grp, d, q)
        copy = remote(split.at[cores[q]], shard(half, vox), probe_send.at[place], probe_recv.at[place], to)
        start(copy, not_first if half else None)
    start(remote(split.at[cores[1]], shard(0, vox), mate_send.at[0], mate_recv.at[0], mate))
    start(remote(pattern, other_pattern, mate_send.at[1], mate_recv.at[1], mate))
    start(remote(noise, other_noise, mate_send.at[2], mate_recv.at[2], mate))
    panels[pl.ds(vox * held, held)] = split[core]

    def prepare(r, carry):
        for n in range(count):
            scale = lax.shift_left(jnp.int32(1), scale_exp[n, r] + 2).astype(jnp.float32) * 0.25
            scaled[r, :, n * width : (n + 1) * width] = (
                blocks[r, n].astype(jnp.float32) * scale
            ).astype(jnp.bfloat16)
        return carry

    lax.fori_loop(0, rows_here, prepare, 0, unroll=2)
    start(remote(
        scaled.at[pl.ds(0, rows_here)], scaled.at[pl.ds(rows_here, rows_here)],
        mate_send.at[3], mate_recv.at[3], mate,
    ))

    def widen(ref, base):
        def one(r, carry):
            weights[base + r] = jnp.transpose(jnp.broadcast_to(ref[pl.ds(r, 1), :], (part, width)))
            return carry

        lax.fori_loop(0, rows_here, one, 0, unroll=2)

    widen(noise, 0)
    remote(pattern, other_pattern, mate_send.at[1], mate_recv.at[1], mate).wait_recv()
    remote(noise, other_noise, mate_send.at[2], mate_recv.at[2], mate).wait_recv()
    widen(other_noise, rows_here)

    both = 2 * entries
    columns = jnp.concatenate([ref[n : n + 1, :] for ref in (pattern, other_pattern) for n in range(count)], axis=1)
    square = jnp.broadcast_to(columns, (both, both))
    turned = jnp.transpose(square)
    row_id = lax.broadcasted_iota(jnp.int32, (both, both), 0)
    lane_id = lax.broadcasted_iota(jnp.int32, (both, both), 1)

    def turn(place):
        second = (place >= entries).astype(jnp.int32)
        within = place - second * entries
        n = sum((within >= m * rows_here).astype(jnp.int32) for m in range(1, count))
        return second * entries + (within - n * rows_here) * count + n

    row_turn, lane_turn = turn(row_id), turn(lane_id)
    tables[0:1] = jnp.max(
        jnp.where((turned == square) & (row_turn < lane_turn), row_turn, -1), axis=0, keepdims=True
    )
    tables[1:2] = jnp.max(jnp.where(turned == lane_id, row_turn, -1), axis=0, keepdims=True)
    tables[2:3] = columns
    tables[3:8] = jnp.zeros((5, both), jnp.int32)
    to_scalars = pltpu.make_async_copy(tables, numbers, local_sem)
    to_scalars.start()
    to_scalars.wait()

    slot = shard(0, vox_at(0, 1))
    remote(slot, slot, mate_send.at[0], mate_recv.at[0], mate).wait_recv()
    slot = scaled.at[pl.ds(rows_here, rows_here)]
    remote(slot, slot, mate_send.at[3], mate_recv.at[3], mate).wait_recv()
    for place, (half, d, q) in enumerate(places):
        slot = shard(half, vox_at(-d, q))
        copy = remote(slot, slot, probe_send.at[place], probe_recv.at[place], mate)
        when(not_last if half else None, copy.wait_recv)

    def row(r, carry):
        left = scaled[r]
        first = lax.div(r, rows_here) * entries + lax.rem(r, rows_here)
        numbered = [first + n * rows_here for n in range(count)]
        picked = jnp.concatenate([panels[numbers[2, i]] for i in numbered], axis=0)
        forward = jnp.dot(left, picked, preferred_element_type=jnp.float32)
        weighted = (weights[r] * forward).astype(jnp.bfloat16)
        back = lax.dot_general(
            left, weighted, (((0,), (0,)), ((), ())), preferred_element_type=jnp.float32
        )
        for n in range(count):
            link = numbers[0, numbered[n]]
            earlier = jnp.where(link >= 0, chain[jnp.maximum(link, 0)], 0.0)
            chain[r * count + n] = back[n * width : (n + 1) * width] + earlier
        return carry

    lax.fori_loop(0, 2 * rows_here, row, 0, unroll=4)

    def total(half, index, k):
        link = numbers[1, (half * voxes + index) * held + k]
        return jnp.where(link >= 0, chain[jnp.maximum(link, 0)], 0.0)

    for place, (half, d, q) in enumerate(places):
        for k in range(held):
            far_out[place, k] = total(half, vox_at(d, q), k).astype(jnp.bfloat16)
        to = device(after if half else grp, d, q)
        copy = remote(far_out.at[place], far_in.at[place], far_send.at[place], far_recv.at[place], to)
        start(copy, not_last if half else None)
    for k in range(held):
        pair_out[k] = total(0, vox_at(0, 1), k)
    start(remote(pair_out, pair_in, mate_send.at[4], mate_recv.at[4], mate))
    remote(pair_out, pair_in, mate_send.at[4], mate_recv.at[4], mate).wait_recv()
    for place, (half, d, q) in enumerate(places):
        copy = remote(far_out.at[place], far_in.at[place], far_send.at[place], far_recv.at[place], mate)
        when(not_first if half else None, copy.wait_recv)
    for k in range(held):
        sums = [total(0, vox, k), pair_in[k]]
        for place, (half, _, q) in enumerate(places):
            arrived = far_in[place, k].astype(jnp.float32)
            sums[q] = sums[q] + (jnp.where(not_first, arrived, 0.0) if half else arrived)
        out[core, k] = sums[0]
        out[1 - core, k] = sums[1]
    for condition, copy in started:
        when(condition, copy.wait_send)


def solution(mesh):
    groups, voxes = mesh.shape["grp"], mesh.shape["vox"]

    def local(probes, blocks, pattern, scale_exp, noise):
        rows_here, count, width, _ = blocks.shape
        cols = probes.shape[1]
        part = cols // 2
        held = probes.shape[0] // width
        entries = rows_here * count
        ys = voxes // 2
        apart = 4 * ys - 2
        smem = pl.BlockSpec(memory_space=pltpu.SMEM)
        vmem = pl.BlockSpec(memory_space=pltpu.VMEM)
        dma = pltpu.SemaphoreType.DMA
        result = pl.pallas_call(
            functools.partial(kernel, groups, voxes),
            out_shape=jax.ShapeDtypeStruct((2, held, width, part), jnp.float32),
            in_specs=[smem] + [vmem] * 4,
            out_specs=vmem,
            scratch_shapes=[
                pltpu.VMEM((2 * voxes * held, width, part), jnp.bfloat16),
                pltpu.VMEM((2, held, width, part), jnp.bfloat16),
                pltpu.VMEM((2 * rows_here, width, count * width), jnp.bfloat16),
                pltpu.VMEM((2 * rows_here, width, part), jnp.float32),
                pltpu.VMEM((2 * entries, width, part), jnp.float32),
                pltpu.VMEM((8, 2 * entries), jnp.int32),
                pltpu.VMEM((count, rows_here), jnp.int32),
                pltpu.VMEM(noise.shape, jnp.float32),
                pltpu.SMEM((8, 2 * entries), jnp.int32),
                pltpu.VMEM((held, width, part), jnp.float32),
                pltpu.VMEM((held, width, part), jnp.float32),
                pltpu.VMEM((apart, held, width, part), jnp.bfloat16),
                pltpu.VMEM((apart, held, width, part), jnp.bfloat16),
                dma((apart,)), dma((apart,)),
                dma((5,)), dma((5,)),
                dma((apart,)), dma((apart,)),
                dma,
            ],
            compiler_params=pltpu.CompilerParams(
                collective_id=0, has_side_effects=True, vmem_limit_bytes=56 * 1024 * 1024
            ),
        )(scale_exp.T, pattern.T, probes.reshape(held, width, cols), blocks, noise)
        halves = result.reshape(2, held * width, part)
        return jnp.concatenate([halves[0], halves[1]], axis=1)

    in_specs = (
        P(("cohort", "grp", "vox"), None),
        P(("cohort", "grp", "vox"), None, None, None),
        P(("cohort", "grp", "vox"), None),
        P(("cohort", "grp", "vox"), None),
        P(("cohort", "grp", "vox"), None),
    )
    out_specs = P(("cohort", "grp", "vox"), None)
    return jax.shard_map(local, mesh=mesh, in_specs=in_specs, out_specs=out_specs, check_vma=False)
```
